256 devices in a mesh: worker: 16 (over z, x_hi), fsdp: 8 (over y, core), tensor: 2 (over x_lo).
Axes of the slice: x: 4 (x_hi: 2, x_lo: 2; x = x_hi * 2 + x_lo), y: 4, z: 8, core: 2. Of those that a mesh axis runs over, the one named last changes fastest.
Arguments:
- tokens: bfloat16 [16, 1024, 2048], P('worker', 'fsdp', 'tensor'), may hold values from -6 to 6
- hidden_grad: bfloat16 [16, 1024, 7168], P('worker', None, ('fsdp', 'tensor')), may hold values from -6 to 6
- local_weights: bfloat16 [16, 2048, 2, 7168], P('worker', None, None, ('fsdp', 'tensor')), may hold values from -6 to 6
- anchor: float32 [2048, 2, 7168], P('worker', None, ('fsdp', 'tensor')), may hold values from -6 to 6
- momentum: float32 [2048, 2, 7168], P('worker', None, ('fsdp', 'tensor')), may hold values from -3 to 3
Outputs:
- updated: bfloat16 [16, 2048, 2, 7168], P('worker', None, None, ('fsdp', 'tensor'))
- anchor_out: float32 [2048, 2, 7168], P('worker', None, ('fsdp', 'tensor'))
- momentum_out: float32 [2048, 2, 7168], P('worker', None, ('fsdp', 'tensor'))
The draws below stay inside these ranges and needn't reach their ends.
All inputs are finite; a program needn't handle non-finite values.
Results may differ from the reference program's by a relative error of at most 0.012.
Values may be sent and summed in bfloat16 or wider, within the bound.
A program may use at most 64 MiB of HBM per device.

```python
import math
import jax
import jax.numpy as jnp
from jax import lax

D = 2048
FF = 7168
WORKERS = 16
TOKW = 1024


def raised(entries, stream_key, source, target, blocks, factor):
    owner, partner = [(jnp.arange(entries.shape[dim]) // (entries.shape[dim] // blocks)).reshape([-1 if axis == dim else 1 for axis in range(entries.ndim)]) for dim in (source, target)]
    chosen = jax.random.permutation(stream_key, blocks)[partner]
    strong = (owner == chosen) | (owner == (partner + blocks // 2) % blocks)
    return jnp.where(strong, factor * entries, entries)


def steps_of(stream_key, extent, shards, least, high):
    level = 1.0
    for position, blocks in shards:
        heights = jax.random.uniform(jax.random.fold_in(jax.random.fold_in(stream_key, 6), position), (blocks,), jnp.float32, least / len(shards), high / len(shards))
        level = level * jnp.repeat(jnp.exp(heights), extent[position] // blocks).reshape((-1,) + (1,) * (len(extent) - 1 - position))
    return level


def normal_values(rng, extent, spread, limit, split=(), kind=jnp.bfloat16):
    values = spread * jax.random.normal(rng, extent, jnp.float32)
    if split:
        values = values * steps_of(rng, extent, split, -0.22, 0.18)
    return jnp.clip(values, -limit, limit).astype(kind)


def gaussian_with(key, extent, deviation, most, pieces, heavy, kind=jnp.bfloat16):
    values = deviation * jax.random.normal(key, extent, jnp.float32)
    if pieces:
        values = values * steps_of(key, extent, pieces, -0.22, 0.18)
    return jnp.clip(raised(values, jax.random.fold_in(key, 3), *heavy), -most, most).astype(kind)


def setup_inputs(seed: int = 0) -> dict:
    key_of = jax.random.split(jax.random.key(seed), 6)
    return {
        "tokens": normal_values(key_of[0], (WORKERS, TOKW, D), 1.0, 6.0, ((0, 16), (1, 8), (2, 2))),
        "hidden_grad": normal_values(key_of[1], (WORKERS, TOKW, FF), 1.0, 6.0, ((0, 16), (2, 16))),
        "local_weights": gaussian_with(key_of[2], (WORKERS, D, 2, FF), 1.0, 6.0, ((0, 16), (3, 16)), (0, 1, 16, 2.0)),
        "anchor": normal_values(key_of[3], (D, 2, FF), 1.0, 6.0, ((0, 16), (2, 16)), jnp.float32),
        "momentum": normal_values(key_of[4], (D, 2, FF), 0.5, 3.0, ((0, 16), (2, 16)), jnp.float32),
    }


MIX_SHARE = 0.5
MOMENTUM_RATE = 0.9
OUTER_RATE = 0.7
INNER_RATE = 1.0

def pair_grad(gate_up, grad_rows):
    gate_part = gate_up[:, 0, :]
    up_part = gate_up[:, 1, :]
    sigmoid_gate = jax.nn.sigmoid(gate_part)
    upstream = grad_rows.astype(jnp.float32)
    grad_gate = upstream * up_part * sigmoid_gate * (1.0 + gate_part * (1.0 - sigmoid_gate))
    grad_up = upstream * gate_part * sigmoid_gate
    return jnp.stack([grad_gate, grad_up], axis=1).astype(jnp.bfloat16)

def reference(tokens, hidden_grad, local_weights, anchor, momentum):

    def accumulate(summed, block):
        return (summed + block.astype(jnp.float32), None)
    summed, _ = lax.scan(accumulate, jnp.zeros(anchor.shape, jnp.float32), local_weights)
    pseudo_grad = anchor - summed / WORKERS
    momentum_out = MOMENTUM_RATE * momentum + pseudo_grad
    anchor_out = anchor - OUTER_RATE * (pseudo_grad + MOMENTUM_RATE * momentum_out)
    anchor_half = anchor_out.astype(jnp.bfloat16).reshape(D, 2 * FF)
    scaling = 1.0 / math.sqrt(D)

    def worker_step(inputs):
        tok_rows, grad_rows, weights_now = inputs
        weight_flat = weights_now.reshape(D, 2 * FF)
        own_part = jnp.dot(tok_rows, weight_flat, preferred_element_type=jnp.float32)
        outer_part = jnp.dot(tok_rows, anchor_half, preferred_element_type=jnp.float32)
        gate_up = (MIX_SHARE * own_part + (1.0 - MIX_SHARE) * outer_part) * scaling
        grad_pair = pair_grad(gate_up.reshape(TOKW, 2, FF), grad_rows).reshape(TOKW, 2 * FF)
        weight_grad = lax.dot_general(tok_rows, grad_pair, (((0,), (0,)), ((), ())), preferred_element_type=jnp.float32) * scaling
        merged = MIX_SHARE * weight_flat.astype(jnp.float32) + (1.0 - MIX_SHARE) * anchor_half.astype(jnp.float32)
        return (merged - INNER_RATE * weight_grad).astype(jnp.bfloat16).reshape(D, 2, FF)
    updated = lax.map(worker_step, (tokens, hidden_grad, local_weights))
    return (updated, anchor_out, momentum_out)
```

```python
import functools
import math

import jax
import jax.numpy as jnp
from jax import lax
from jax.experimental import pallas as pl
from jax.experimental.pallas import tpu as pltpu
from jax.sharding import PartitionSpec as P

MIX = 0.5
MOMENTUM_RATE = 0.9
OUTER_RATE = 0.7
D = 2048
FFL = 448
TOK = 1024
WORKERS = 16
SCALE = 1.0 / math.sqrt(D)
F32 = jnp.float32
BF16 = jnp.bfloat16
MESH = pl.DeviceIdType.MESH

CHUNKS = [
    (64, 1, 1, 3), (64, 0, 1, 4), (64, 1, 0, 3), (64, 0, 0, 4),
    (64, 1, 1, 3), (64, 0, 1, 4), (64, 1, 0, 3),
]
ORDER = [
    (-1, 0), (0, 0), (1, -1), (2, 0), (3, -1), (4, 0), (5, -1), (6, 0), (0, 1), (2, 1),
    (4, 1), (-1, 1), (6, 1), (0, 2), (2, 2), (4, 2), (-1, 2), (6, 2), (1, 0), (0, 3),
    (2, 3), (4, 3), (6, 3), (3, 0), (1, 1), (0, 4), (2, 4), (4, 4), (-1, 3), (5, 0),
    (6, 4), (-1, 5), (0, 5), (1, 2), (2, 5), (3, 1), (4, 5), (5, 1), (0, 7), (6, 5),
    (1, 3), (3, 2), (2, 6), (4, 7), (5, 2), (0, 8), (1, 5), (3, 3), (6, 6), (2, 7),
    (4, 8), (5, 3), (0, 9), (1, 7), (3, 5), (6, 7), (2, 8), (0, 10), (4, 9), (5, 5),
    (-1, 6), (1, 8), (3, 6), (6, 8), (-1, 4), (0, 11), (2, 9), (4, 10), (0, 12), (1, 9),
    (5, 7), (0, 13), (3, 7), (4, 11), (1, 10), (6, 9), (4, 12), (5, 8), (4, 13), (3, 8),
    (2, 11), (2, 12), (5, 9), (2, 13), (3, 9), (1, 11), (1, 12), (5, 10), (1, 13), (6, 11),
    (6, 12), (6, 13), (3, 11), (3, 12), (3, 13), (5, 11), (5, 12), (5, 13),
]


def kernel(tok, hgt, wt, ant, mot, upt, aot, mut,
           x_v, wz, an, mo, hg, rsr, rss, rsr1, rss1, xr, xs, xr8, az, own, mb, gp, ov,
           lsem, osem, gs, gr, rs_s, rs_r, ag_s, ag_r, xx_s, xx_r, ax_s, ax_r):
    w = lax.axis_index("worker")
    f = lax.axis_index("fsdp")
    t = lax.axis_index("tensor")
    z, xh, y, core = w // 2, w % 2, f // 2, f % 2
    xo = 1 - xh

    def dev(dz=0, dx=0, dy=0, dc=0, dt=0):
        return (((z + dz + 8) % 8) * 2 + (xh + dx) % 2,
                ((y + dy + 4) % 4) * 2 + (core + dc) % 2, (t + dt) % 2)

    zdev = (dev(dz=1), dev(dz=-1))
    xdev = dev(dx=1)
    ydevs = (dev(dy=1), dev(dy=-1), dev(dy=2))
    cdev = dev(dc=1)
    tdev = dev(dt=1)

    barrier = pltpu.get_barrier_semaphore()
    for d in (*zdev, xdev, *ydevs, cdev, tdev):
        pl.semaphore_signal(barrier, inc=1, device_id=d, device_id_type=MESH)

    loads = []

    def load(src, dst, k):
        c = pltpu.make_async_copy(src, dst, lsem.at[k])
        c.start()
        loads.append(c)

    def rowblock(ff):
        return pl.ds(pl.multiple_of(ff * 128, 128), 128)

    def colblock(tt):
        return pl.ds(pl.multiple_of(tt * 1024, 128), 1024)

    load(tok, x_v.at[rowblock(f), colblock(t)], 0)
    for zz in range(8):
        load(wt.at[:, :, pl.ds(zz * 256, 256)], wz.at[zz], 1 + zz)
    load(ant, an, 9)
    load(mot, mo, 10)
    load(hgt, hg, 11)
    for c in loads[:9]:
        c.wait()

    pl.semaphore_wait(barrier, 8)

    sent = []

    def copy(src, dst, ssem, rsem, to):
        return pltpu.make_async_remote_copy(src_ref=src, dst_ref=dst, send_sem=ssem, recv_sem=rsem,
                                            device_id=to, device_id_type=MESH)

    def send(src, dst, ssem, rsem, to):
        c = copy(src, dst, ssem, rsem, to)
        c.start()
        sent.append(c)

    def arrived(ref, rsem):
        copy(ref, ref, ssem=gs.at[0], rsem=rsem, to=cdev).wait_recv()

    def piece(ff, tt):
        return x_v.at[rowblock(ff), colblock(tt)]

    to = 1 - t
    fy = [((y + dy + 4) % 4) * 2 + core for dy in (-1, 1, -2)]

    def g_own():
        p = piece(f, t)
        send(p, p, gs.at[0], gr.at[0], tdev)
        for k in range(3):
            send(p, p, gs.at[1 + k], gr.at[1 + k], ydevs[k])
        send(p, p, gs.at[4], gr.at[4], cdev)

    def g_pair():
        p = piece(f, to)
        arrived(p, gr.at[0])
        for k in range(3):
            send(p, p, gs.at[5 + k], gr.at[5 + k], ydevs[k])
        send(p, p, gs.at[8], gr.at[8], cdev)

    def g_y(tt, k0, k1):
        for k in range(3):
            p = piece(fy[k], tt)
            arrived(p, gr.at[k0 + k])
            send(p, p, gs.at[k1 + k], gr.at[k1 + k], cdev)

    def g_end():
        fo = f + 1 - 2 * core
        arrived(piece(fo, t), gr.at[4])
        arrived(piece(fo, to), gr.at[8])
        for k in range(3):
            ff = fy[k] + 1 - 2 * core
            arrived(piece(ff, t), gr.at[9 + k])
            arrived(piece(ff, to), gr.at[12 + k])

    starts = [sum(r[0] for r in CHUNKS[:i]) for i in range(len(CHUNKS))]

    def lanes(h):
        return pl.ds(pl.multiple_of(h * 128, 128), 128)

    def zof(k):
        return (z + k + 16) % 8

    def run(c, name):
        R, rz, az_first, up = CHUNKS[c]
        rows = pl.ds(starts[c], R)
        dirs = ((0, 1, up), (1, -1, 7 - up))

        def f32(ref):
            return ref[...].astype(F32)

        if name == -1:
            send(wz.at[:, :, rows, lanes(xo)], xr8.at[:, :, rows], xx_s.at[c], xx_r.at[c], xdev)
        elif 0 <= name <= 3:
            s = name
            if not rz and s == 0:
                arrived(xr8.at[:, :, rows], xx_r.at[c])
            for d, sg, n in dirs:
                if s >= n:
                    continue
                zo = zof(sg * (n - s))
                k = d * 4 + s
                if rz:
                    src = wz.at[zo, :, rows]
                    if s > 0:
                        got = rsr.at[k - 1, :, rows]
                        arrived(got, rs_r.at[c, k - 1])
                        rss[k, :, rows] = (f32(src) + f32(got)).astype(BF16)
                        src = rss.at[k, :, rows]
                    send(src, rsr.at[k, :, rows], rs_s.at[c, k], rs_r.at[c, k], zdev[d])
                else:
                    total = f32(wz.at[zo, :, rows, lanes(xh)]) + f32(xr8.at[zo, :, rows])
                    if s > 0:
                        got = rsr1.at[k - 1, :, rows]
                        arrived(got, rs_r.at[c, k - 1])
                        total = total + f32(got)
                    rss1[k, :, rows] = total.astype(BF16)
                    send(rss1.at[k, :, rows], rsr1.at[k, :, rows], rs_s.at[c, k], rs_r.at[c, k], zdev[d])
        elif name == 4:
            for d, sg, n in dirs:
                arrived(rsr.at[d * 4 + n - 1, :, rows], rs_r.at[c, d * 4 + n - 1])

            def part(h):
                return (f32(wz.at[z, :, rows, lanes(h)]) + f32(rsr.at[up - 1, :, rows, lanes(h)])
                        + f32(rsr.at[4 + 6 - up, :, rows, lanes(h)]))

            xs[:, rows] = part(xo).astype(BF16)
            send(xs.at[:, rows], xr.at[:, rows], xx_s.at[c], xx_r.at[c], xdev)
            own[:, rows] = part(xh)
        elif name == 5:
            if rz:
                arrived(xr.at[:, rows], xx_r.at[c])
                total = own[:, rows] + f32(xr.at[:, rows])
            else:
                for d, sg, n in dirs:
                    arrived(rsr1.at[d * 4 + n - 1, :, rows], rs_r.at[c, d * 4 + n - 1])
                total = (f32(wz.at[z, :, rows, lanes(xh)]) + f32(xr8.at[z, :, rows])
                         + f32(rsr1.at[up - 1, :, rows]) + f32(rsr1.at[4 + 6 - up, :, rows]))
            anchor = an[:, rows]
            pseudo = anchor - total * (1.0 / WORKERS)
            mom = MOMENTUM_RATE * mo[:, rows] + pseudo
            new = anchor - OUTER_RATE * (pseudo + MOMENTUM_RATE * mom)
            mo[:, rows] = mom
            an[:, rows] = new
            az[z, xh, :, rows] = new.astype(BF16)
            mine = az.at[z, xh, :, rows]
            send(mine, mine, ax_s.at[c, 0], ax_r.at[c], xdev)
            if az_first:
                for d, sg, n in dirs:
                    send(mine, mine, ag_s.at[c, d * 4], ag_r.at[c, d * 4], zdev[d])
        elif 6 <= name <= 10:
            s = name - 6
            if not az_first and s == 0:
                arrived(az.at[z, xo, :, rows], ax_r.at[c])
            for d, sg, n in dirs:
                if s > n or (s == n and not az_first):
                    continue
                zo = zof(-sg * s)
                if az_first:
                    blk = az.at[zo, xh, :, rows]
                else:
                    blk = az.at[zo, :, :, rows]
                if s > 0:
                    arrived(blk, ag_r.at[c, d * 4 + s - 1])
                if s < n:
                    send(blk, blk, ag_s.at[c, d * 4 + s], ag_r.at[c, d * 4 + s], zdev[d])
                if az_first:
                    send(blk, blk, ax_s.at[c, d * up + s], ax_r.at[c], xdev)
        elif name == 11:
            if az_first:
                arrived(az.at[:, xo, :, rows], ax_r.at[c])
            else:
                for d, sg, n in dirs:
                    arrived(az.at[zof(-sg * n), :, :, rows], ag_r.at[c, d * 4 + n - 1])

            @pl.loop(0, 8)
            def _(zz):
                for h in range(2):
                    for p in range(2):
                        m = MIX * f32(wz.at[zz, p, rows, pl.ds(h * 128, 128)]) + (1.0 - MIX) * f32(az.at[zz, h, p, rows])
                        mb[pl.ds(p * R, R), pl.ds(pl.multiple_of(zz * 256 + h * 128, 128), 128)] = m.astype(BF16)
        elif name == 12:
            @pl.loop(0, 4)
            def _(i):
                tk = pl.ds(pl.multiple_of(i * 256, 256), 256)
                g = lax.dot_general(mb[pl.ds(0, 2 * R), :], x_v[tk, :], (((1,), (1,)), ((), ())),
                                    preferred_element_type=F32) * SCALE
                gate, upp = g[:R], g[R:]
                up_g = hg[rows, tk].astype(F32)
                sig = jax.nn.sigmoid(gate)
                gs_ = up_g * sig
                gp[pl.ds(0, R), tk] = (gs_ * upp * (1.0 + gate * (1.0 - sig))).astype(BF16)
                gp[pl.ds(R, R), tk] = (gs_ * gate).astype(BF16)
        elif name == 13:
            @pl.loop(0, 8)
            def _(zz):
                cols = pl.ds(pl.multiple_of(zz * 256, 256), 256)
                wg = jnp.dot(gp[pl.ds(0, 2 * R), :], x_v[:, cols], preferred_element_type=F32) * SCALE
                for p in range(2):
                    for h in range(2):
                        m = MIX * f32(wz.at[zz, p, rows, pl.ds(h * 128, 128)]) + (1.0 - MIX) * f32(az.at[zz, h, p, rows])
                        ov[p, rows, pl.ds(pl.multiple_of(zz * 256 + h * 128, 128), 128)] = (
                            m - wg[p * R:(p + 1) * R, h * 128:(h + 1) * 128]).astype(BF16)
            pltpu.make_async_copy(ov.at[:, rows], upt.at[:, rows], osem.at[c]).start()

    for c, name in ORDER:
        if c >= 0:
            run(c, name)
        elif name == 0:
            g_own()
        elif name == 1:
            g_pair()
        elif name == 2:
            g_y(t, 1, 9)
        elif name == 3:
            g_y(to, 5, 12)
        elif name == 4:
            g_end()
            loads[11].wait()
        elif name == 5:
            for l in loads[9:11]:
                l.wait()
        elif name == 6:
            pltpu.make_async_copy(an, aot, osem.at[len(CHUNKS)]).start()
            pltpu.make_async_copy(mo, mut, osem.at[len(CHUNKS) + 1]).start()

    for s in sent:
        s.wait_send()
    for c in range(len(CHUNKS)):
        rows = pl.ds(starts[c], CHUNKS[c][0])
        pltpu.make_async_copy(ov.at[:, rows], upt.at[:, rows], osem.at[c]).wait()
    pltpu.make_async_copy(an, aot, osem.at[len(CHUNKS)]).wait()
    pltpu.make_async_copy(mo, mut, osem.at[len(CHUNKS) + 1]).wait()


def body(tokens, hidden_grad, local_weights, anchor, momentum):
    n = len(CHUNKS)
    most = max(r[0] for r in CHUNKS)
    dma = pltpu.SemaphoreType.DMA
    hbm = pl.BlockSpec(memory_space=pl.ANY)
    up, an, mo = pl.pallas_call(
        kernel,
        name="outer_inner_step",
        out_shape=(
            jax.ShapeDtypeStruct((2, FFL, D), BF16),
            jax.ShapeDtypeStruct((2, FFL, 128), F32),
            jax.ShapeDtypeStruct((2, FFL, 128), F32),
        ),
        in_specs=[hbm] * 5,
        out_specs=(hbm,) * 3,
        scratch_shapes=[
            pltpu.VMEM((TOK, D), BF16),
            pltpu.VMEM((8, 2, FFL, 256), BF16),
            pltpu.VMEM((2, FFL, 128), F32),
            pltpu.VMEM((2, FFL, 128), F32),
            pltpu.VMEM((FFL, TOK), BF16),
            pltpu.VMEM((8, 2, FFL, 256), BF16),
            pltpu.VMEM((8, 2, FFL, 256), BF16),
            pltpu.VMEM((8, 2, FFL, 128), BF16),
            pltpu.VMEM((8, 2, FFL, 128), BF16),
            pltpu.VMEM((2, FFL, 128), BF16),
            pltpu.VMEM((2, FFL, 128), BF16),
            pltpu.VMEM((8, 2, FFL, 128), BF16),
            pltpu.VMEM((8, 2, 2, FFL, 128), BF16),
            pltpu.VMEM((2, FFL, 128), F32),
            pltpu.VMEM((2 * most, D), BF16),
            pltpu.VMEM((2 * most, TOK), BF16),
            pltpu.VMEM((2, FFL, D), BF16),
            dma((12,)),
            dma((n + 2,)),
            dma((15,)), dma((15,)),
            dma((n, 8)), dma((n, 8)),
            dma((n, 8)), dma((n, 8)),
            dma((n,)), dma((n,)),
            dma((n, 8)), dma((n,)),
        ],
        compiler_params=pltpu.CompilerParams(
            collective_id=0, has_side_effects=True, vmem_limit_bytes=56 << 20),
        cost_estimate=pl.CostEstimate(flops=4 * TOK * 2 * FFL * D, bytes_accessed=11_000_000, transcendentals=TOK * FFL),
    )(
        tokens[0],
        hidden_grad[0].T,
        local_weights[0].transpose(1, 2, 0),
        anchor.transpose(1, 2, 0),
        momentum.transpose(1, 2, 0),
    )
    return (up.transpose(2, 0, 1)[None], an.transpose(2, 0, 1), mo.transpose(2, 0, 1))


def solution(mesh):
    in_specs = (
        P("worker", "fsdp", "tensor"),
        P("worker", None, ("fsdp", "tensor")),
        P("worker", None, None, ("fsdp", "tensor")),
        P("worker", None, ("fsdp", "tensor")),
        P("worker", None, ("fsdp", "tensor")),
    )
    out_specs = (
        P("worker", None, None, ("fsdp", "tensor")),
        P("worker", None, ("fsdp", "tensor")),
        P("worker", None, ("fsdp", "tensor")),
    )
    return jax.shard_map(body, mesh=mesh, in_specs=in_specs, out_specs=out_specs, check_vma=False)
```

```python
import functools
import math

import jax
import jax.numpy as jnp
from jax import lax
from jax.experimental import pallas as pl
from jax.experimental.pallas import tpu as pltpu
from jax.sharding import PartitionSpec as P

MIX = 0.5
MOMENTUM_RATE = 0.9
OUTER_RATE = 0.7
D = 2048
FFL = 448
TOK = 1024
WORKERS = 16
SCALE = 1.0 / math.sqrt(D)
F32 = jnp.float32
BF16 = jnp.bfloat16
MESH = pl.DeviceIdType.MESH

CHUNKS = [
    (48, 1, 1, 3), (48, 1, 1, 4), (80, 0, 1, 3), (80, 1, 1, 3),
    (48, 0, 0, 4), (32, 1, 0, 4), (64, 1, 0, 4), (48, 0, 1, 4),
]
ORDER = [
    (-1, 0), (0, 0), (1, 0), (2, -1), (3, 0), (0, 1), (1, 1), (4, -1), (5, 0), (3, 1),
    (-1, 1), (0, 2), (1, 2), (5, 1), (3, 2), (0, 3), (1, 3), (5, 2), (-1, 2), (6, 0),
    (3, 3), (2, 0), (0, 4), (1, 4), (5, 3), (7, -1), (6, 1), (4, 0), (5, 4), (-1, 5),
    (0, 5), (1, 5), (2, 1), (3, 4), (6, 2), (4, 1), (0, 7), (1, 7), (2, 2), (-1, 3),
    (7, 0), (5, 5), (6, 3), (4, 2), (0, 8), (3, 5), (1, 8), (2, 3), (7, 1), (5, 6),
    (6, 4), (4, 3), (0, 9), (3, 7), (2, 5), (1, 9), (7, 2), (5, 7), (6, 5), (0, 10),
    (4, 5), (3, 8), (2, 7), (1, 10), (7, 3), (5, 8), (3, 9), (6, 6), (2, 8), (-1, 4),
    (0, 11), (7, 5), (5, 9), (4, 6), (0, 12), (3, 10), (0, 13), (6, 7), (2, 9), (1, 11),
    (7, 7), (1, 12), (1, 13), (4, 7), (5, 11), (5, 12), (6, 8), (2, 10), (5, 13), (7, 8),
    (3, 11), (4, 8), (3, 12), (6, 9), (3, 13), (7, 9), (2, 11), (4, 9), (2, 12), (2, 13),
    (7, 10), (6, 11), (6, 12), (6, 13), (4, 11), (4, 12), (4, 13), (7, 11), (7, 12), (7, 13),
]


def kernel(tok, hgt, wt, ant, mot, ov, an, mo,
           x_v, wz, hg, rsr, rss, rsr1, rss1, xr, xs, xr8, az, own, mb, gp,
           lsem, gs, gr, rs_s, rs_r, ag_s, ag_r, xx_s, xx_r, ax_s, ax_r):
    w = lax.axis_index("worker")
    f = lax.axis_index("fsdp")
    t = lax.axis_index("tensor")
    z, xh, y, core = w // 2, w % 2, f // 2, f % 2
    xo = 1 - xh

    def dev(dz=0, dx=0, dy=0, dc=0, dt=0):
        return (((z + dz + 8) % 8) * 2 + (xh + dx) % 2,
                ((y + dy + 4) % 4) * 2 + (core + dc) % 2, (t + dt) % 2)

    zdev = (dev(dz=1), dev(dz=-1))
    xdev = dev(dx=1)
    ydevs = (dev(dy=1), dev(dy=-1), dev(dy=2))
    cdev = dev(dc=1)
    tdev = dev(dt=1)

    barrier = pltpu.get_barrier_semaphore()
    for d in (*zdev, xdev, *ydevs, cdev, tdev):
        pl.semaphore_signal(barrier, inc=1, device_id=d, device_id_type=MESH)

    loads = []

    def load(src, dst, k):
        c = pltpu.make_async_copy(src, dst, lsem.at[k])
        c.start()
        loads.append(c)

    def rowblock(ff):
        return pl.ds(pl.multiple_of(ff * 128, 128), 128)

    def colblock(tt):
        return pl.ds(pl.multiple_of(tt * 1024, 128), 1024)

    load(tok, x_v.at[rowblock(f), colblock(t)], 0)
    for zz in range(8):
        load(wt.at[:, :, pl.ds(zz * 256, 256)], wz.at[zz], 1 + zz)
    load(ant, an, 9)
    load(mot, mo, 10)
    load(hgt, hg, 11)
    pl.semaphore_wait(barrier, 8)
    waited = []

    def need(*ks):
        for k in ks:
            if k not in waited:
                waited.append(k)
                loads[k].wait()

    sent = []

    def copy(src, dst, ssem, rsem, to):
        return pltpu.make_async_remote_copy(src_ref=src, dst_ref=dst, send_sem=ssem, recv_sem=rsem,
                                            device_id=to, device_id_type=MESH)

    def send(src, dst, ssem, rsem, to):
        c = copy(src, dst, ssem, rsem, to)
        c.start()
        sent.append(c)

    def arrived(ref, rsem):
        copy(ref, ref, ssem=gs.at[0], rsem=rsem, to=cdev).wait_recv()

    def piece(ff, tt):
        return x_v.at[rowblock(ff), colblock(tt)]

    to = 1 - t
    fy = [((y + dy + 4) % 4) * 2 + core for dy in (-1, 1, -2)]

    def g_own():
        p = piece(f, t)
        send(tok, p, gs.at[0], gr.at[0], tdev)
        for k in range(3):
            send(tok, p, gs.at[1 + k], gr.at[1 + k], ydevs[k])
        send(tok, p, gs.at[4], gr.at[4], cdev)

    def g_pair():
        p = piece(f, to)
        arrived(p, gr.at[0])
        for k in range(3):
            send(p, p, gs.at[5 + k], gr.at[5 + k], ydevs[k])
        send(p, p, gs.at[8], gr.at[8], cdev)

    def g_y(tt, k0, k1):
        for k in range(3):
            p = piece(fy[k], tt)
            arrived(p, gr.at[k0 + k])
            send(p, p, gs.at[k1 + k], gr.at[k1 + k], cdev)

    def g_end():
        fo = f + 1 - 2 * core
        arrived(piece(fo, t), gr.at[4])
        arrived(piece(fo, to), gr.at[8])
        for k in range(3):
            ff = fy[k] + 1 - 2 * core
            arrived(piece(ff, t), gr.at[9 + k])
            arrived(piece(ff, to), gr.at[12 + k])

    starts = [sum(r[0] for r in CHUNKS[:i]) for i in range(len(CHUNKS))]

    def lanes(h):
        return pl.ds(pl.multiple_of(h * 128, 128), 128)

    def zof(k):
        return (z + k + 16) % 8

    def run(c, name):
        R, rz, az_first, up = CHUNKS[c]
        rows = pl.ds(starts[c], R)
        dirs = ((0, 1, up), (1, -1, 7 - up))

        def f32(ref):
            return ref[...].astype(F32)

        if name == 0 and rz:
            pass
        else:
            need(*range(1, 9))
        if name == -1:
            send(wz.at[:, :, rows, lanes(xo)], xr8.at[:, :, rows], xx_s.at[c], xx_r.at[c], xdev)
        elif 0 <= name <= 3:
            s = name
            if not rz and s == 0:
                arrived(xr8.at[:, :, rows], xx_r.at[c])
            for d, sg, n in dirs:
                if s >= n:
                    continue
                zo = zof(sg * (n - s))
                k = d * 4 + s
                if rz:
                    src = wz.at[zo, :, rows]
                    if s == 0:
                        src = wt.at[:, rows, pl.ds(pl.multiple_of(zo * 256, 256), 256)]
                    else:
                        got = rsr.at[k - 1, :, rows]
                        arrived(got, rs_r.at[c, k - 1])
                        rss[k, :, rows] = (f32(src) + f32(got)).astype(BF16)
                        src = rss.at[k, :, rows]
                    send(src, rsr.at[k, :, rows], rs_s.at[c, k], rs_r.at[c, k], zdev[d])
                else:
                    total = f32(wz.at[zo, :, rows, lanes(xh)]) + f32(xr8.at[zo, :, rows])
                    if s > 0:
                        got = rsr1.at[k - 1, :, rows]
                        arrived(got, rs_r.at[c, k - 1])
                        total = total + f32(got)
                    rss1[k, :, rows] = total.astype(BF16)
                    send(rss1.at[k, :, rows], rsr1.at[k, :, rows], rs_s.at[c, k], rs_r.at[c, k], zdev[d])
        elif name == 4:
            for d, sg, n in dirs:
                arrived(rsr.at[d * 4 + n - 1, :, rows], rs_r.at[c, d * 4 + n - 1])

            def part(h):
                return (f32(wz.at[z, :, rows, lanes(h)]) + f32(rsr.at[up - 1, :, rows, lanes(h)])
                        + f32(rsr.at[4 + 6 - up, :, rows, lanes(h)]))

            xs[:, rows] = part(xo).astype(BF16)
            send(xs.at[:, rows], xr.at[:, rows], xx_s.at[c], xx_r.at[c], xdev)
            own[:, rows] = part(xh)
        elif name == 5:
            if rz:
                arrived(xr.at[:, rows], xx_r.at[c])
                total = own[:, rows] + f32(xr.at[:, rows])
            else:
                for d, sg, n in dirs:
                    arrived(rsr1.at[d * 4 + n - 1, :, rows], rs_r.at[c, d * 4 + n - 1])
                total = (f32(wz.at[z, :, rows, lanes(xh)]) + f32(xr8.at[z, :, rows])
                         + f32(rsr1.at[up - 1, :, rows]) + f32(rsr1.at[4 + 6 - up, :, rows]))
            anchor = an[:, rows]
            pseudo = anchor - total * (1.0 / WORKERS)
            mom = MOMENTUM_RATE * mo[:, rows] + pseudo
            new = anchor - OUTER_RATE * (pseudo + MOMENTUM_RATE * mom)
            mo[:, rows] = mom
            an[:, rows] = new
            az[z, xh, :, rows] = new.astype(BF16)
            mine = az.at[z, xh, :, rows]
            send(mine, mine, ax_s.at[c, 0], ax_r.at[c], xdev)
            if az_first:
                for d, sg, n in dirs:
                    send(mine, mine, ag_s.at[c, d * 4], ag_r.at[c, d * 4], zdev[d])
        elif 6 <= name <= 10:
            s = name - 6
            if not az_first and s == 0:
                arrived(az.at[z, xo, :, rows], ax_r.at[c])
            for d, sg, n in dirs:
                if s > n or (s == n and not az_first):
                    continue
                zo = zof(-sg * s)
                if az_first:
                    blk = az.at[zo, xh, :, rows]
                else:
                    blk = az.at[zo, :, :, rows]
                if s > 0:
                    arrived(blk, ag_r.at[c, d * 4 + s - 1])
                if s < n:
                    send(blk, blk, ag_s.at[c, d * 4 + s], ag_r.at[c, d * 4 + s], zdev[d])
                if az_first:
                    send(blk, blk, ax_s.at[c, d * up + s], ax_r.at[c], xdev)
        elif name == 11:
            if az_first:
                arrived(az.at[:, xo, :, rows], ax_r.at[c])
            else:
                for d, sg, n in dirs:
                    arrived(az.at[zof(-sg * n), :, :, rows], ag_r.at[c, d * 4 + n - 1])

            for zz in range(8):
                for h in range(2):
                    for p in range(2):
                        m = MIX * f32(wz.at[zz, p, rows, pl.ds(h * 128, 128)]) + (1.0 - MIX) * f32(az.at[zz, h, p, rows])
                        mb[pl.ds(p * R, R), pl.ds(zz * 256 + h * 128, 128)] = m.astype(BF16)
        elif name == 12:
            for i in range(4):
                tk = pl.ds(i * 256, 256)
                g = lax.dot_general(mb[pl.ds(0, 2 * R), :], x_v[tk, :], (((1,), (1,)), ((), ())),
                                    preferred_element_type=F32) * SCALE
                gate, upp = g[:R], g[R:]
                up_g = hg[rows, tk].astype(F32)
                sig = jax.nn.sigmoid(gate)
                gs_ = up_g * sig
                gp[pl.ds(0, R), tk] = (gs_ * upp * (1.0 + gate * (1.0 - sig))).astype(BF16)
                gp[pl.ds(R, R), tk] = (gs_ * gate).astype(BF16)
        elif name == 13:
            for zz in range(8):
                cols = pl.ds(zz * 256, 256)
                wg = jnp.dot(gp[pl.ds(0, 2 * R), :], x_v[:, cols], preferred_element_type=F32) * SCALE
                for p in range(2):
                    for h in range(2):
                        m = MIX * f32(wz.at[zz, p, rows, pl.ds(h * 128, 128)]) + (1.0 - MIX) * f32(az.at[zz, h, p, rows])
                        ov[p, rows, pl.ds(zz * 256 + h * 128, 128)] = (
                            m - wg[p * R:(p + 1) * R, h * 128:(h + 1) * 128]).astype(BF16)

    for c, name in ORDER:
        if c >= 0:
            run(c, name)
        elif name == 0:
            g_own()
        elif name == 1:
            g_pair()
        elif name == 2:
            g_y(t, 1, 9)
        elif name == 3:
            g_y(to, 5, 12)
        elif name == 4:
            g_end()
            need(0, 11)
        elif name == 5:
            need(9, 10)

    for s in sent:
        s.wait_send()


def store(ov, an, mo, upt, aot, mut, sem):
    copies = [pltpu.make_async_copy(src, dst, sem.at[k])
              for k, (src, dst) in enumerate(((ov, upt), (an, aot), (mo, mut)))]
    for c in copies:
        c.start()
    for c in copies:
        c.wait()


def body(tokens, hidden_grad, local_weights, anchor, momentum):
    n = len(CHUNKS)
    most = max(r[0] for r in CHUNKS)
    dma = pltpu.SemaphoreType.DMA
    hbm = pl.BlockSpec(memory_space=pl.ANY)
    up, an, mo = pl.pallas_call(
        kernel,
        name="outer_inner_step",
        out_shape=(
            pltpu.VMEM((2, FFL, D), BF16),
            pltpu.VMEM((2, FFL, 128), F32),
            pltpu.VMEM((2, FFL, 128), F32),
        ),
        in_specs=[hbm] * 5,
        out_specs=(pl.BlockSpec(memory_space=pltpu.VMEM),) * 3,
        scratch_shapes=[
            pltpu.VMEM((TOK, D), BF16),
            pltpu.VMEM((8, 2, FFL, 256), BF16),
            pltpu.VMEM((FFL, TOK), BF16),
            pltpu.VMEM((8, 2, FFL, 256), BF16),
            pltpu.VMEM((8, 2, FFL, 256), BF16),
            pltpu.VMEM((8, 2, FFL, 128), BF16),
            pltpu.VMEM((8, 2, FFL, 128), BF16),
            pltpu.VMEM((2, FFL, 128), BF16),
            pltpu.VMEM((2, FFL, 128), BF16),
            pltpu.VMEM((8, 2, FFL, 128), BF16),
            pltpu.VMEM((8, 2, 2, FFL, 128), BF16),
            pltpu.VMEM((2, FFL, 128), F32),
            pltpu.VMEM((2 * most, D), BF16),
            pltpu.VMEM((2 * most, TOK), BF16),
            dma((12,)),
            dma((15,)), dma((15,)),
            dma((n, 8)), dma((n, 8)),
            dma((n, 8)), dma((n, 8)),
            dma((n,)), dma((n,)),
            dma((n, 8)), dma((n,)),
        ],
        compiler_params=pltpu.CompilerParams(
            collective_id=0, has_side_effects=True, vmem_limit_bytes=52 << 20),
        cost_estimate=pl.CostEstimate(flops=4 * TOK * 2 * FFL * D, bytes_accessed=11_000_000, transcendentals=TOK * FFL),
    )(
        tokens[0],
        hidden_grad[0].T,
        local_weights[0].transpose(1, 2, 0),
        anchor.transpose(1, 2, 0),
        momentum.transpose(1, 2, 0),
    )
    up, an, mo = pl.pallas_call(
        store,
        name="store",
        out_shape=(
            jax.ShapeDtypeStruct((2, FFL, D), BF16),
            jax.ShapeDtypeStruct((2, FFL, 128), F32),
            jax.ShapeDtypeStruct((2, FFL, 128), F32),
        ),
        in_specs=[pl.BlockSpec(memory_space=pltpu.VMEM)] * 3,
        out_specs=(hbm,) * 3,
        scratch_shapes=[dma((3,))],
        compiler_params=pltpu.CompilerParams(vmem_limit_bytes=8 << 20),
    )(*(pltpu.with_memory_space_constraint(a, pltpu.VMEM) for a in (up, an, mo)))
    return (up.transpose(2, 0, 1)[None], an.transpose(2, 0, 1), mo.transpose(2, 0, 1))


def solution(mesh):
    in_specs = (
        P("worker", "fsdp", "tensor"),
        P("worker", None, ("fsdp", "tensor")),
        P("worker", None, None, ("fsdp", "tensor")),
        P("worker", None, ("fsdp", "tensor")),
        P("worker", None, ("fsdp", "tensor")),
    )
    out_specs = (
        P("worker", None, None, ("fsdp", "tensor")),
        P("worker", None, ("fsdp", "tensor")),
        P("worker", None, ("fsdp", "tensor")),
    )
    return jax.shard_map(body, mesh=mesh, in_specs=in_specs, out_specs=out_specs, check_vma=False)
```

```python
import functools
import math

import jax
import jax.numpy as jnp
from jax import lax
from jax.experimental import pallas as pl
from jax.experimental.pallas import tpu as pltpu
from jax.sharding import PartitionSpec as P

MIX = 0.5
MOMENTUM_RATE = 0.9
OUTER_RATE = 0.7
D = 2048
FFL = 448
TOK = 1024
WORKERS = 16
SCALE = 1.0 / math.sqrt(D)
F32 = jnp.float32
BF16 = jnp.bfloat16
MESH = pl.DeviceIdType.MESH

CHUNKS = [
    (48, 1, 1, 3), (48, 1, 1, 4), (80, 0, 1, 3), (80, 1, 1, 3),
    (48, 0, 0, 4), (32, 1, 0, 4), (64, 1, 0, 4), (48, 0, 1, 4),
]
ORDER = [
    (-1, 0), (0, 0), (1, 0), (2, -1), (3, 0), (0, 1), (1, 1), (4, -1), (5, 0), (3, 1),
    (-1, 1), (0, 2), (1, 2), (5, 1), (3, 2), (0, 3), (1, 3), (5, 2), (-1, 2), (6, 0),
    (3, 3), (2, 0), (0, 4), (1, 4), (5, 3), (7, -1), (6, 1), (4, 0), (5, 4), (-1, 5),
    (0, 5), (1, 5), (2, 1), (3, 4), (6, 2), (4, 1), (0, 7), (1, 7), (2, 2), (-1, 3),
    (7, 0), (5, 5), (6, 3), (4, 2), (0, 8), (3, 5), (1, 8), (2, 3), (7, 1), (-1, 4),
    (5, 6), (-1, 8), (6, 4), (4, 3), (0, 9), (-1, 9), (3, 7), (-1, 10), (2, 5), (1, 9),
    (-1, 11), (7, 2), (5, 7), (6, 5), (0, 10), (4, 5), (3, 8), (2, 7), (1, 10), (7, 3),
    (5, 8), (3, 9), (6, 6), (2, 8), (0, 11), (7, 5), (5, 9), (4, 6), (0, 12), (3, 10),
    (0, 13), (6, 7), (2, 9), (1, 11), (7, 7), (1, 12), (1, 13), (4, 7), (5, 11), (5, 12),
    (6, 8), (2, 10), (5, 13), (7, 8), (3, 11), (4, 8), (3, 12), (6, 9), (3, 13), (7, 9),
    (2, 11), (4, 9), (2, 12), (2, 13), (7, 10), (6, 11), (6, 12), (6, 13), (4, 11), (4, 12),
    (4, 13), (7, 11), (7, 12), (7, 13),
]


def kernel(tok, hgt, wt, ant, mot, ov, an, mo,
           x_v, wz, hg, rsr, rss, rsr1, rss1, xr, xs, xr8, az, own, mb, gp, xt,
           lsem, gs, gr, rs_s, rs_r, ag_s, ag_r, xx_s, xx_r, ax_s, ax_r):
    w = lax.axis_index("worker")
    f = lax.axis_index("fsdp")
    t = lax.axis_index("tensor")
    z, xh, y, core = w // 2, w % 2, f // 2, f % 2
    xo = 1 - xh

    def dev(dz=0, dx=0, dy=0, dc=0, dt=0):
        return (((z + dz + 8) % 8) * 2 + (xh + dx) % 2,
                ((y + dy + 4) % 4) * 2 + (core + dc) % 2, (t + dt) % 2)

    zdev = (dev(dz=1), dev(dz=-1))
    xdev = dev(dx=1)
    ydevs = (dev(dy=1), dev(dy=-1), dev(dy=2))
    cdev = dev(dc=1)
    tdev = dev(dt=1)

    barrier = pltpu.get_barrier_semaphore()
    for d in (*zdev, xdev, *ydevs, cdev, tdev):
        pl.semaphore_signal(barrier, inc=1, device_id=d, device_id_type=MESH)

    loads = []

    def load(src, dst, k):
        c = pltpu.make_async_copy(src, dst, lsem.at[k])
        c.start()
        loads.append(c)

    def rowblock(ff):
        return pl.ds(pl.multiple_of(ff * 128, 128), 128)

    def colblock(tt):
        return pl.ds(pl.multiple_of(tt * 1024, 128), 1024)

    load(tok, x_v.at[rowblock(f), colblock(t)], 0)
    for zz in range(8):
        load(wt.at[:, :, pl.ds(zz * 256, 256)], wz.at[zz], 1 + zz)
    load(ant, an, 9)
    load(mot, mo, 10)
    load(hgt, hg, 11)
    pl.semaphore_wait(barrier, 8)
    waited = []

    def need(*ks):
        for k in ks:
            if k not in waited:
                waited.append(k)
                loads[k].wait()

    sent = []

    def copy(src, dst, ssem, rsem, to):
        return pltpu.make_async_remote_copy(src_ref=src, dst_ref=dst, send_sem=ssem, recv_sem=rsem,
                                            device_id=to, device_id_type=MESH)

    def send(src, dst, ssem, rsem, to):
        c = copy(src, dst, ssem, rsem, to)
        c.start()
        sent.append(c)

    def arrived(ref, rsem):
        copy(ref, ref, ssem=gs.at[0], rsem=rsem, to=cdev).wait_recv()

    def piece(ff, tt):
        return x_v.at[rowblock(ff), colblock(tt)]

    to = 1 - t
    fy = [((y + dy + 4) % 4) * 2 + core for dy in (-1, 1, -2)]

    def g_own():
        p = piece(f, t)
        send(tok, p, gs.at[0], gr.at[0], tdev)
        for k in range(3):
            send(tok, p, gs.at[1 + k], gr.at[1 + k], ydevs[k])
        send(tok, p, gs.at[4], gr.at[4], cdev)

    def g_pair():
        p = piece(f, to)
        arrived(p, gr.at[0])
        for k in range(3):
            send(p, p, gs.at[5 + k], gr.at[5 + k], ydevs[k])
        send(p, p, gs.at[8], gr.at[8], cdev)

    def g_y(tt, k0, k1):
        for k in range(3):
            p = piece(fy[k], tt)
            arrived(p, gr.at[k0 + k])
            send(p, p, gs.at[k1 + k], gr.at[k1 + k], cdev)

    def g_end():
        fo = f + 1 - 2 * core
        arrived(piece(fo, t), gr.at[4])
        arrived(piece(fo, to), gr.at[8])
        for k in range(3):
            ff = fy[k] + 1 - 2 * core
            arrived(piece(ff, t), gr.at[9 + k])
            arrived(piece(ff, to), gr.at[12 + k])

    starts = [sum(r[0] for r in CHUNKS[:i]) for i in range(len(CHUNKS))]

    def lanes(h):
        return pl.ds(pl.multiple_of(h * 128, 128), 128)

    def zof(k):
        return (z + k + 16) % 8

    def run(c, name):
        R, rz, az_first, up = CHUNKS[c]
        rows = pl.ds(starts[c], R)
        dirs = ((0, 1, up), (1, -1, 7 - up))

        def f32(ref):
            return ref[...].astype(F32)

        if name == 0 and rz:
            pass
        else:
            need(*range(1, 9))
        if name == -1:
            send(wz.at[:, :, rows, lanes(xo)], xr8.at[:, :, rows], xx_s.at[c], xx_r.at[c], xdev)
        elif 0 <= name <= 3:
            s = name
            if not rz and s == 0:
                arrived(xr8.at[:, :, rows], xx_r.at[c])
            for d, sg, n in dirs:
                if s >= n:
                    continue
                zo = zof(sg * (n - s))
                k = d * 4 + s
                if rz:
                    src = wz.at[zo, :, rows]
                    if s == 0:
                        src = wt.at[:, rows, pl.ds(pl.multiple_of(zo * 256, 256), 256)]
                    else:
                        got = rsr.at[k - 1, :, rows]
                        arrived(got, rs_r.at[c, k - 1])
                        rss[k, :, rows] = (f32(src) + f32(got)).astype(BF16)
                        src = rss.at[k, :, rows]
                    send(src, rsr.at[k, :, rows], rs_s.at[c, k], rs_r.at[c, k], zdev[d])
                else:
                    total = f32(wz.at[zo, :, rows, lanes(xh)]) + f32(xr8.at[zo, :, rows])
                    if s > 0:
                        got = rsr1.at[k - 1, :, rows]
                        arrived(got, rs_r.at[c, k - 1])
                        total = total + f32(got)
                    rss1[k, :, rows] = total.astype(BF16)
                    send(rss1.at[k, :, rows], rsr1.at[k, :, rows], rs_s.at[c, k], rs_r.at[c, k], zdev[d])
        elif name == 4:
            for d, sg, n in dirs:
                arrived(rsr.at[d * 4 + n - 1, :, rows], rs_r.at[c, d * 4 + n - 1])

            def part(h):
                return (f32(wz.at[z, :, rows, lanes(h)]) + f32(rsr.at[up - 1, :, rows, lanes(h)])
                        + f32(rsr.at[4 + 6 - up, :, rows, lanes(h)]))

            xs[:, rows] = part(xo).astype(BF16)
            send(xs.at[:, rows], xr.at[:, rows], xx_s.at[c], xx_r.at[c], xdev)
            own[:, rows] = part(xh)
        elif name == 5:
            if rz:
                arrived(xr.at[:, rows], xx_r.at[c])
                total = own[:, rows] + f32(xr.at[:, rows])
            else:
                for d, sg, n in dirs:
                    arrived(rsr1.at[d * 4 + n - 1, :, rows], rs_r.at[c, d * 4 + n - 1])
                total = (f32(wz.at[z, :, rows, lanes(xh)]) + f32(xr8.at[z, :, rows])
                         + f32(rsr1.at[up - 1, :, rows]) + f32(rsr1.at[4 + 6 - up, :, rows]))
            anchor = an[:, rows]
            pseudo = anchor - total * (1.0 / WORKERS)
            mom = MOMENTUM_RATE * mo[:, rows] + pseudo
            new = anchor - OUTER_RATE * (pseudo + MOMENTUM_RATE * mom)
            mo[:, rows] = mom
            an[:, rows] = new
            az[z, xh, :, rows] = new.astype(BF16)
            mine = az.at[z, xh, :, rows]
            send(mine, mine, ax_s.at[c, 0], ax_r.at[c], xdev)
            if az_first:
                for d, sg, n in dirs:
                    send(mine, mine, ag_s.at[c, d * 4], ag_r.at[c, d * 4], zdev[d])
        elif 6 <= name <= 10:
            s = name - 6
            if not az_first and s == 0:
                arrived(az.at[z, xo, :, rows], ax_r.at[c])
            for d, sg, n in dirs:
                if s > n or (s == n and not az_first):
                    continue
                zo = zof(-sg * s)
                if az_first:
                    blk = az.at[zo, xh, :, rows]
                else:
                    blk = az.at[zo, :, :, rows]
                if s > 0:
                    arrived(blk, ag_r.at[c, d * 4 + s - 1])
                if s < n:
                    send(blk, blk, ag_s.at[c, d * 4 + s], ag_r.at[c, d * 4 + s], zdev[d])
                if az_first:
                    send(blk, blk, ax_s.at[c, d * up + s], ax_r.at[c], xdev)
        elif name == 11:
            if az_first:
                arrived(az.at[:, xo, :, rows], ax_r.at[c])
            else:
                for d, sg, n in dirs:
                    arrived(az.at[zof(-sg * n), :, :, rows], ag_r.at[c, d * 4 + n - 1])

            for zz in range(8):
                for h in range(2):
                    for p in range(2):
                        m = MIX * f32(wz.at[zz, p, rows, pl.ds(h * 128, 128)]) + (1.0 - MIX) * f32(az.at[zz, h, p, rows])
                        mb[pl.ds(p * R, R), pl.ds(zz * 256 + h * 128, 128)] = m.astype(BF16)
        elif name == 12:
            for i in range(4):
                tk = pl.ds(i * 256, 256)
                g = jnp.dot(mb[pl.ds(0, 2 * R), :], xt[:, tk], preferred_element_type=F32) * SCALE
                gate, upp = g[:R], g[R:]
                up_g = hg[rows, tk].astype(F32)
                sig = jax.nn.sigmoid(gate)
                gs_ = up_g * sig
                gp[pl.ds(0, R), tk] = (gs_ * upp * (1.0 + gate * (1.0 - sig))).astype(BF16)
                gp[pl.ds(R, R), tk] = (gs_ * gate).astype(BF16)
        elif name == 13:
            for zz in range(8):
                cols = pl.ds(zz * 256, 256)
                wg = jnp.dot(gp[pl.ds(0, 2 * R), :], x_v[:, cols], preferred_element_type=F32) * SCALE
                for p in range(2):
                    for h in range(2):
                        m = MIX * f32(wz.at[zz, p, rows, pl.ds(h * 128, 128)]) + (1.0 - MIX) * f32(az.at[zz, h, p, rows])
                        ov[p, rows, pl.ds(zz * 256 + h * 128, 128)] = (
                            m - wg[p * R:(p + 1) * R, h * 128:(h + 1) * 128]).astype(BF16)

    for c, name in ORDER:
        if c >= 0:
            run(c, name)
        elif name == 0:
            g_own()
        elif name == 1:
            g_pair()
        elif name == 2:
            g_y(t, 1, 9)
        elif name == 3:
            g_y(to, 5, 12)
        elif name == 4:
            g_end()
            need(0, 11)
        elif name == 5:
            need(9, 10)
        elif name >= 8:
            for i in (2 * name - 16, 2 * name - 15):
                xt[:, pl.ds(i * 128, 128)] = x_v[pl.ds(i * 128, 128), :].T

    for s in sent:
        s.wait_send()


def store(ov, an, mo, upt, aot, mut, sem):
    copies = [pltpu.make_async_copy(src, dst, sem.at[k])
              for k, (src, dst) in enumerate(((ov, upt), (an, aot), (mo, mut)))]
    for c in copies:
        c.start()
    for c in copies:
        c.wait()


def body(tokens, hidden_grad, local_weights, anchor, momentum):
    n = len(CHUNKS)
    most = max(r[0] for r in CHUNKS)
    dma = pltpu.SemaphoreType.DMA
    hbm = pl.BlockSpec(memory_space=pl.ANY)
    up, an, mo = pl.pallas_call(
        kernel,
        name="outer_inner_step",
        out_shape=(
            pltpu.VMEM((2, FFL, D), BF16),
            pltpu.VMEM((2, FFL, 128), F32),
            pltpu.VMEM((2, FFL, 128), F32),
        ),
        in_specs=[hbm] * 5,
        out_specs=(pl.BlockSpec(memory_space=pltpu.VMEM),) * 3,
        scratch_shapes=[
            pltpu.VMEM((TOK, D), BF16),
            pltpu.VMEM((8, 2, FFL, 256), BF16),
            pltpu.VMEM((FFL, TOK), BF16),
            pltpu.VMEM((8, 2, FFL, 256), BF16),
            pltpu.VMEM((8, 2, FFL, 256), BF16),
            pltpu.VMEM((8, 2, FFL, 128), BF16),
            pltpu.VMEM((8, 2, FFL, 128), BF16),
            pltpu.VMEM((2, FFL, 128), BF16),
            pltpu.VMEM((2, FFL, 128), BF16),
            pltpu.VMEM((8, 2, FFL, 128), BF16),
            pltpu.VMEM((8, 2, 2, FFL, 128), BF16),
            pltpu.VMEM((2, FFL, 128), F32),
            pltpu.VMEM((2 * most, D), BF16),
            pltpu.VMEM((2 * most, TOK), BF16),
            pltpu.VMEM((D, TOK), BF16),
            dma((12,)),
            dma((15,)), dma((15,)),
            dma((n, 8)), dma((n, 8)),
            dma((n, 8)), dma((n, 8)),
            dma((n,)), dma((n,)),
            dma((n, 8)), dma((n,)),
        ],
        compiler_params=pltpu.CompilerParams(
            collective_id=0, has_side_effects=True, vmem_limit_bytes=52 << 20),
        cost_estimate=pl.CostEstimate(flops=4 * TOK * 2 * FFL * D, bytes_accessed=11_000_000, transcendentals=TOK * FFL),
    )(
        tokens[0],
        hidden_grad[0].T,
        local_weights[0].transpose(1, 2, 0),
        anchor.transpose(1, 2, 0),
        momentum.transpose(1, 2, 0),
    )
    up, an, mo = pl.pallas_call(
        store,
        name="store",
        out_shape=(
            jax.ShapeDtypeStruct((2, FFL, D), BF16),
            jax.ShapeDtypeStruct((2, FFL, 128), F32),
            jax.ShapeDtypeStruct((2, FFL, 128), F32),
        ),
        in_specs=[pl.BlockSpec(memory_space=pltpu.VMEM)] * 3,
        out_specs=(hbm,) * 3,
        scratch_shapes=[dma((3,))],
        compiler_params=pltpu.CompilerParams(vmem_limit_bytes=8 << 20),
    )(*(pltpu.with_memory_space_constraint(a, pltpu.VMEM) for a in (up, an, mo)))
    return (up.transpose(2, 0, 1)[None], an.transpose(2, 0, 1), mo.transpose(2, 0, 1))


def solution(mesh):
    in_specs = (
        P("worker", "fsdp", "tensor"),
        P("worker", None, ("fsdp", "tensor")),
        P("worker", None, None, ("fsdp", "tensor")),
        P("worker", None, ("fsdp", "tensor")),
        P("worker", None, ("fsdp", "tensor")),
    )
    out_specs = (
        P("worker", None, None, ("fsdp", "tensor")),
        P("worker", None, ("fsdp", "tensor")),
        P("worker", None, ("fsdp", "tensor")),
    )
    return jax.shard_map(body, mesh=mesh, in_specs=in_specs, out_specs=out_specs, check_vma=False)
```

```python
import functools
import math

import jax
import jax.numpy as jnp
from jax import lax
from jax.experimental import pallas as pl
from jax.experimental.pallas import tpu as pltpu
from jax.sharding import PartitionSpec as P

MIX = 0.5
MOMENTUM_RATE = 0.9
OUTER_RATE = 0.7
D = 2048
FFL = 448
TOK = 1024
WORKERS = 16
SCALE = 1.0 / math.sqrt(D)
F32 = jnp.float32
BF16 = jnp.bfloat16
MESH = pl.DeviceIdType.MESH

CHUNKS = [
    (32, 1, 1, 3), (96, 0, 0, 3), (80, 0, 1, 4), (48, 1, 1, 4),
    (48, 1, 1, 4), (64, 1, 1, 3), (80, 1, 0, 4),
]
ORDER = [
    (-1, 0), (0, 0), (1, -1), (2, -1), (3, 0), (4, 0), (5, 0), (6, 0), (0, 1), (3, 1),
    (4, 1), (-1, 1), (5, 1), (6, 1), (0, 2), (3, 2), (4, 2), (5, 2), (-1, 2), (1, 0),
    (6, 2), (0, 3), (3, 3), (4, 3), (5, 3), (1, 1), (6, 3), (2, 0), (0, 4), (3, 4),
    (4, 4), (5, 4), (-1, 3), (1, 2), (-1, 5), (0, 5), (6, 4), (3, 5), (2, 1), (4, 5),
    (5, 5), (-1, 4), (1, 3), (-1, 8), (0, 7), (3, 7), (-1, 9), (6, 5), (2, 2), (-1, 10),
    (4, 7), (5, 7), (-1, 11), (1, 5), (0, 8), (3, 8), (2, 3), (6, 6), (4, 8), (5, 8),
    (0, 9), (3, 9), (2, 5), (1, 6), (6, 7), (4, 9), (0, 10), (5, 9), (3, 10), (2, 7),
    (1, 7), (6, 8), (5, 10), (0, 11), (4, 10), (0, 12), (2, 8), (0, 13), (3, 11), (1, 8),
    (3, 12), (3, 13), (6, 9), (5, 11), (5, 12), (2, 9), (5, 13), (1, 9), (4, 11), (4, 12),
    (4, 13), (6, 11), (6, 12), (2, 10), (6, 13), (1, 11), (1, 12), (1, 13), (2, 11), (2, 12),
    (2, 13),
]

LAST = [c for c, step in ORDER if c >= 0 and step == 11][-1]
FIRST_ROW = sum(r[0] for r in CHUNKS[:LAST])
LAST_ROWS = CHUNKS[LAST][0]


def pair_grad(g, up_g, R):
    gate, upp = g[:R], g[R:]
    sig = jax.nn.sigmoid(gate)
    scaled = up_g * sig
    return (scaled * upp * (1.0 + gate * (1.0 - sig))).astype(BF16), (scaled * gate).astype(BF16)


def kernel(tok, hgt, wt, ant, mot, ov, an, mo, x_v, xt, mbl, mfl, hg,
           wz, rsr, rss, rsr1, rss1, xr, xs, xr8, az, own, mb, gp,
           lsem, gs, gr, rs_s, rs_r, ag_s, ag_r, xx_s, xx_r, ax_s, ax_r):
    w = lax.axis_index("worker")
    f = lax.axis_index("fsdp")
    t = lax.axis_index("tensor")
    z, xh, y, core = w // 2, w % 2, f // 2, f % 2
    xo = 1 - xh

    def dev(dz=0, dx=0, dy=0, dc=0, dt=0):
        return (((z + dz + 8) % 8) * 2 + (xh + dx) % 2,
                ((y + dy + 4) % 4) * 2 + (core + dc) % 2, (t + dt) % 2)

    zdev = (dev(dz=1), dev(dz=-1))
    xdev = dev(dx=1)
    ydevs = (dev(dy=1), dev(dy=-1), dev(dy=2))
    cdev = dev(dc=1)
    tdev = dev(dt=1)

    barrier = pltpu.get_barrier_semaphore()
    for d in (*zdev, xdev, *ydevs, cdev, tdev):
        pl.semaphore_signal(barrier, inc=1, device_id=d, device_id_type=MESH)

    loads = []

    def load(src, dst, k):
        c = pltpu.make_async_copy(src, dst, lsem.at[k])
        c.start()
        loads.append(c)

    def rowblock(ff):
        return pl.ds(pl.multiple_of(ff * 128, 128), 128)

    def colblock(tt):
        return pl.ds(pl.multiple_of(tt * 1024, 128), 1024)

    load(tok, x_v.at[rowblock(f), colblock(t)], 0)
    for zz in range(8):
        load(wt.at[:, :, pl.ds(zz * 256, 256)], wz.at[zz], 1 + zz)
    load(ant, an, 9)
    load(mot, mo, 10)
    load(hgt, hg, 11)
    pl.semaphore_wait(barrier, 8)
    waited = []

    def need(*ks):
        for k in ks:
            if k not in waited:
                waited.append(k)
                loads[k].wait()

    sent = []

    def copy(src, dst, ssem, rsem, to):
        return pltpu.make_async_remote_copy(src_ref=src, dst_ref=dst, send_sem=ssem, recv_sem=rsem,
                                            device_id=to, device_id_type=MESH)

    def send(src, dst, ssem, rsem, to):
        c = copy(src, dst, ssem, rsem, to)
        c.start()
        sent.append(c)

    def arrived(ref, rsem):
        copy(ref, ref, ssem=gs.at[0], rsem=rsem, to=cdev).wait_recv()

    def piece(ff, tt):
        return x_v.at[rowblock(ff), colblock(tt)]

    to = 1 - t
    fy = [((y + dy + 4) % 4) * 2 + core for dy in (-1, 1, -2)]

    def g_own():
        p = piece(f, t)
        send(tok, p, gs.at[0], gr.at[0], tdev)
        for k in range(3):
            send(tok, p, gs.at[1 + k], gr.at[1 + k], ydevs[k])
        send(tok, p, gs.at[4], gr.at[4], cdev)

    def g_pair():
        p = piece(f, to)
        arrived(p, gr.at[0])
        for k in range(3):
            send(p, p, gs.at[5 + k], gr.at[5 + k], ydevs[k])
        send(p, p, gs.at[8], gr.at[8], cdev)

    def g_y(tt, k0, k1):
        for k in range(3):
            p = piece(fy[k], tt)
            arrived(p, gr.at[k0 + k])
            send(p, p, gs.at[k1 + k], gr.at[k1 + k], cdev)

    def g_end():
        fo = f + 1 - 2 * core
        arrived(piece(fo, t), gr.at[4])
        arrived(piece(fo, to), gr.at[8])
        for k in range(3):
            ff = fy[k] + 1 - 2 * core
            arrived(piece(ff, t), gr.at[9 + k])
            arrived(piece(ff, to), gr.at[12 + k])

    starts = [sum(r[0] for r in CHUNKS[:i]) for i in range(len(CHUNKS))]

    def lanes(h):
        return pl.ds(pl.multiple_of(h * 128, 128), 128)

    def zof(k):
        return (z + k + 16) % 8

    def run(c, name):
        R, rz, az_first, up = CHUNKS[c]
        rows = pl.ds(starts[c], R)
        dirs = ((0, 1, up), (1, -1, 7 - up))

        def f32(ref):
            return ref[...].astype(F32)

        if name == 0 and rz:
            pass
        else:
            need(*range(1, 9))
        if name == -1:
            send(wz.at[:, :, rows, lanes(xo)], xr8.at[:, :, rows], xx_s.at[c], xx_r.at[c], xdev)
        elif 0 <= name <= 3:
            s = name
            if not rz and s == 0:
                arrived(xr8.at[:, :, rows], xx_r.at[c])
            for d, sg, n in dirs:
                if s >= n:
                    continue
                zo = zof(sg * (n - s))
                k = d * 4 + s
                if rz:
                    src = wz.at[zo, :, rows]
                    if s == 0:
                        src = wt.at[:, rows, pl.ds(pl.multiple_of(zo * 256, 256), 256)]
                    else:
                        got = rsr.at[k - 1, :, rows]
                        arrived(got, rs_r.at[c, k - 1])
                        rss[k, :, rows] = (f32(src) + f32(got)).astype(BF16)
                        src = rss.at[k, :, rows]
                    send(src, rsr.at[k, :, rows], rs_s.at[c, k], rs_r.at[c, k], zdev[d])
                else:
                    total = f32(wz.at[zo, :, rows, lanes(xh)]) + f32(xr8.at[zo, :, rows])
                    if s > 0:
                        got = rsr1.at[k - 1, :, rows]
                        arrived(got, rs_r.at[c, k - 1])
                        total = total + f32(got)
                    rss1[k, :, rows] = total.astype(BF16)
                    send(rss1.at[k, :, rows], rsr1.at[k, :, rows], rs_s.at[c, k], rs_r.at[c, k], zdev[d])
        elif name == 4:
            for d, sg, n in dirs:
                arrived(rsr.at[d * 4 + n - 1, :, rows], rs_r.at[c, d * 4 + n - 1])

            def part(h):
                return (f32(wz.at[z, :, rows, lanes(h)]) + f32(rsr.at[up - 1, :, rows, lanes(h)])
                        + f32(rsr.at[4 + 6 - up, :, rows, lanes(h)]))

            xs[:, rows] = part(xo).astype(BF16)
            send(xs.at[:, rows], xr.at[:, rows], xx_s.at[c], xx_r.at[c], xdev)
            own[:, rows] = part(xh)
        elif name == 5:
            if rz:
                arrived(xr.at[:, rows], xx_r.at[c])
                total = own[:, rows] + f32(xr.at[:, rows])
            else:
                for d, sg, n in dirs:
                    arrived(rsr1.at[d * 4 + n - 1, :, rows], rs_r.at[c, d * 4 + n - 1])
                total = (f32(wz.at[z, :, rows, lanes(xh)]) + f32(xr8.at[z, :, rows])
                         + f32(rsr1.at[up - 1, :, rows]) + f32(rsr1.at[4 + 6 - up, :, rows]))
            anchor = an[:, rows]
            pseudo = anchor - total * (1.0 / WORKERS)
            mom = MOMENTUM_RATE * mo[:, rows] + pseudo
            new = anchor - OUTER_RATE * (pseudo + MOMENTUM_RATE * mom)
            mo[:, rows] = mom
            an[:, rows] = new
            az[z, xh, :, rows] = new.astype(BF16)
            mine = az.at[z, xh, :, rows]
            send(mine, mine, ax_s.at[c, 0], ax_r.at[c], xdev)
            if az_first:
                for d, sg, n in dirs:
                    send(mine, mine, ag_s.at[c, d * 4], ag_r.at[c, d * 4], zdev[d])
        elif 6 <= name <= 10:
            s = name - 6
            if not az_first and s == 0:
                arrived(az.at[z, xo, :, rows], ax_r.at[c])
            for d, sg, n in dirs:
                if s > n or (s == n and not az_first):
                    continue
                zo = zof(-sg * s)
                if az_first:
                    blk = az.at[zo, xh, :, rows]
                else:
                    blk = az.at[zo, :, :, rows]
                if s > 0:
                    arrived(blk, ag_r.at[c, d * 4 + s - 1])
                if s < n:
                    send(blk, blk, ag_s.at[c, d * 4 + s], ag_r.at[c, d * 4 + s], zdev[d])
                if az_first:
                    send(blk, blk, ax_s.at[c, d * up + s], ax_r.at[c], xdev)
        elif name == 11:
            if az_first:
                arrived(az.at[:, xo, :, rows], ax_r.at[c])
            else:
                for d, sg, n in dirs:
                    arrived(az.at[zof(-sg * n), :, :, rows], ag_r.at[c, d * 4 + n - 1])

            for zz in range(8):
                for h in range(2):
                    for p in range(2):
                        m = MIX * f32(wz.at[zz, p, rows, pl.ds(h * 128, 128)]) + (1.0 - MIX) * f32(az.at[zz, h, p, rows])
                        to_row, to_col = pl.ds(p * R, R), pl.ds(zz * 256 + h * 128, 128)
                        if c == LAST:
                            mbl[to_row, to_col] = m.astype(BF16)
                            mfl[to_row, to_col] = m
                        else:
                            mb[to_row, to_col] = m.astype(BF16)
        elif name == 12:
            for i in range(4):
                tk = pl.ds(i * 256, 256)
                g = jnp.dot(mb[pl.ds(0, 2 * R), :], xt[:, tk], preferred_element_type=F32) * SCALE
                gp[pl.ds(0, R), tk], gp[pl.ds(R, R), tk] = pair_grad(g, hg[rows, tk].astype(F32), R)
        elif name == 13:
            for zz in range(8):
                cols = pl.ds(zz * 256, 256)
                wg = jnp.dot(gp[pl.ds(0, 2 * R), :], x_v[:, cols], preferred_element_type=F32) * SCALE
                for p in range(2):
                    for h in range(2):
                        m = MIX * f32(wz.at[zz, p, rows, pl.ds(h * 128, 128)]) + (1.0 - MIX) * f32(az.at[zz, h, p, rows])
                        ov[p, rows, pl.ds(zz * 256 + h * 128, 128)] = (
                            m - wg[p * R:(p + 1) * R, h * 128:(h + 1) * 128]).astype(BF16)

    for c, name in ORDER:
        if c == LAST and name > 11:
            continue
        if c >= 0:
            run(c, name)
            for _ in range(min(4, max(0, len(sent) - 40))):
                sent.pop(0).wait_send()
        elif name == 0:
            g_own()
        elif name == 1:
            g_pair()
        elif name == 2:
            g_y(t, 1, 9)
        elif name == 3:
            g_y(to, 5, 12)
        elif name == 4:
            g_end()
            need(0, 11)
        elif name == 5:
            need(9, 10)
        elif name >= 8:
            for i in (2 * name - 16, 2 * name - 15):
                xt[:, pl.ds(i * 128, 128)] = x_v[pl.ds(i * 128, 128), :].T

    for s in sent:
        s.wait_send()


def finish(ov, an, mo, x_v, xt, mbl, mfl, hg, upt, aot, mut, gp, ol, sem):
    R = LAST_ROWS
    end = FIRST_ROW + R
    rows = pl.ds(FIRST_ROW, R)
    moves = [(an, aot), (mo, mut)]
    for lo, n in ((0, FIRST_ROW), (end, FFL - end)):
        if n:
            moves.append((ov.at[:, pl.ds(lo, n)], upt.at[:, pl.ds(lo, n)]))
    copies = [pltpu.make_async_copy(src, dst, sem.at[k]) for k, (src, dst) in enumerate(moves)]
    for c in copies:
        c.start()
    for i in range(4):
        tk = pl.ds(i * 256, 256)
        g = jnp.dot(mbl[...], xt[:, tk], preferred_element_type=F32) * SCALE
        gp[pl.ds(0, R), tk], gp[pl.ds(R, R), tk] = pair_grad(g, hg[rows, tk].astype(F32), R)
    for zz in range(8):
        cols = pl.ds(zz * 256, 256)
        wg = jnp.dot(gp[...], x_v[:, cols], preferred_element_type=F32) * SCALE
        for p in range(2):
            ol[p, :, cols] = (mfl[pl.ds(p * R, R), cols] - wg[p * R:(p + 1) * R]).astype(BF16)
    last = pltpu.make_async_copy(ol, upt.at[:, rows], sem.at[4])
    last.start()
    for c in copies + [last]:
        c.wait()


def body(tokens, hidden_grad, local_weights, anchor, momentum):
    n = len(CHUNKS)
    most = max(r[0] for r in CHUNKS)
    dma = pltpu.SemaphoreType.DMA
    hbm = pl.BlockSpec(memory_space=pl.ANY)
    vmem = pl.BlockSpec(memory_space=pltpu.VMEM)
    held = pl.pallas_call(
        kernel,
        name="outer_inner_step",
        out_shape=(
            pltpu.VMEM((2, FFL, D), BF16),
            pltpu.VMEM((2, FFL, 128), F32),
            pltpu.VMEM((2, FFL, 128), F32),
            pltpu.VMEM((TOK, D), BF16),
            pltpu.VMEM((D, TOK), BF16),
            pltpu.VMEM((2 * LAST_ROWS, D), BF16),
            pltpu.VMEM((2 * LAST_ROWS, D), F32),
            pltpu.VMEM((FFL, TOK), BF16),
        ),
        in_specs=[hbm] * 5,
        out_specs=(vmem,) * 8,
        scratch_shapes=[
            pltpu.VMEM((8, 2, FFL, 256), BF16),
            pltpu.VMEM((8, 2, FFL, 256), BF16),
            pltpu.VMEM((8, 2, FFL, 256), BF16),
            pltpu.VMEM((8, 2, FFL, 128), BF16),
            pltpu.VMEM((8, 2, FFL, 128), BF16),
            pltpu.VMEM((2, FFL, 128), BF16),
            pltpu.VMEM((2, FFL, 128), BF16),
            pltpu.VMEM((8, 2, FFL, 128), BF16),
            pltpu.VMEM((8, 2, 2, FFL, 128), BF16),
            pltpu.VMEM((2, FFL, 128), F32),
            pltpu.VMEM((2 * most, D), BF16),
            pltpu.VMEM((2 * most, TOK), BF16),
            dma((12,)),
            dma((15,)), dma((15,)),
            dma((n, 8)), dma((n, 8)),
            dma((n, 8)), dma((n, 8)),
            dma((n,)), dma((n,)),
            dma((n, 8)), dma((n,)),
        ],
        compiler_params=pltpu.CompilerParams(
            collective_id=0, has_side_effects=True, vmem_limit_bytes=45 << 20),
        cost_estimate=pl.CostEstimate(flops=4 * TOK * 2 * FFL * D, bytes_accessed=11_000_000, transcendentals=TOK * FFL),
    )(
        tokens[0],
        hidden_grad[0].T,
        local_weights[0].transpose(1, 2, 0),
        anchor.transpose(1, 2, 0),
        momentum.transpose(1, 2, 0),
    )
    up, an, mo = pl.pallas_call(
        finish,
        name="finish",
        out_shape=(
            jax.ShapeDtypeStruct((2, FFL, D), BF16),
            jax.ShapeDtypeStruct((2, FFL, 128), F32),
            jax.ShapeDtypeStruct((2, FFL, 128), F32),
        ),
        in_specs=[vmem] * 8,
        out_specs=(hbm,) * 3,
        scratch_shapes=[
            pltpu.VMEM((2 * LAST_ROWS, TOK), BF16),
            pltpu.VMEM((2, LAST_ROWS, D), BF16),
            dma((5,)),
        ],
        compiler_params=pltpu.CompilerParams(vmem_limit_bytes=12 << 20),
    )(*(pltpu.with_memory_space_constraint(a, pltpu.VMEM) for a in held))
    return (up.transpose(2, 0, 1)[None], an.transpose(2, 0, 1), mo.transpose(2, 0, 1))


def solution(mesh):
    in_specs = (
        P("worker", "fsdp", "tensor"),
        P("worker", None, ("fsdp", "tensor")),
        P("worker", None, None, ("fsdp", "tensor")),
        P("worker", None, ("fsdp", "tensor")),
        P("worker", None, ("fsdp", "tensor")),
    )
    out_specs = (
        P("worker", None, None, ("fsdp", "tensor")),
        P("worker", None, ("fsdp", "tensor")),
        P("worker", None, ("fsdp", "tensor")),
    )
    return jax.shard_map(body, mesh=mesh, in_specs=in_specs, out_specs=out_specs, check_vma=False)
```

```python
import functools
import math

import jax
import jax.numpy as jnp
from jax import lax
from jax.experimental import pallas as pl
from jax.experimental.pallas import tpu as pltpu
from jax.sharding import PartitionSpec as P

MIX = 0.5
MOMENTUM_RATE = 0.9
OUTER_RATE = 0.7
D = 2048
FFL = 448
TOK = 1024
WORKERS = 16
SCALE = 1.0 / math.sqrt(D)
F32 = jnp.float32
BF16 = jnp.bfloat16
MESH = pl.DeviceIdType.MESH

CHUNKS = [
    (32, 1, 1, 3), (96, 0, 0, 3), (80, 0, 1, 4), (48, 1, 1, 4),
    (48, 1, 1, 4), (64, 1, 1, 3), (80, 1, 0, 4),
]
ORDER = [
    (-1, 0), (0, 0), (1, -1), (2, -1), (3, 0), (4, 0), (5, 0), (6, 0), (0, 1), (3, 1),
    (4, 1), (-1, 1), (5, 1), (6, 1), (0, 2), (3, 2), (4, 2), (5, 2), (-1, 2), (1, 0),
    (6, 2), (0, 3), (3, 3), (4, 3), (5, 3), (1, 1), (6, 3), (2, 0), (0, 4), (3, 4),
    (4, 4), (5, 4), (-1, 3), (1, 2), (-1, 5), (0, 5), (6, 4), (3, 5), (2, 1), (4, 5),
    (5, 5), (-1, 4), (1, 3), (-1, 8), (0, 7), (3, 7), (-1, 9), (6, 5), (2, 2), (-1, 10),
    (4, 7), (5, 7), (-1, 11), (1, 5), (0, 8), (3, 8), (2, 3), (6, 6), (4, 8), (5, 8),
    (0, 9), (3, 9), (2, 5), (1, 6), (6, 7), (4, 9), (0, 10), (5, 9), (3, 10), (2, 7),
    (1, 7), (6, 8), (5, 10), (0, 11), (4, 10), (0, 12), (2, 8), (0, 13), (3, 11), (1, 8),
    (3, 12), (3, 13), (6, 9), (5, 11), (5, 12), (2, 9), (5, 13), (1, 9), (4, 11), (4, 12),
    (4, 13), (6, 11), (6, 12), (2, 10), (6, 13), (1, 11), (1, 12), (1, 13), (2, 11), (2, 12),
    (2, 13),
]

LAST = [c for c, step in ORDER if c >= 0 and step == 11][-1]
FIRST_ROW = sum(r[0] for r in CHUNKS[:LAST])
LAST_ROWS = CHUNKS[LAST][0]


def pair_grad(g, up_g, R):
    gate, upp = g[:R], g[R:]
    sig = jax.nn.sigmoid(gate)
    scaled = up_g * sig
    return (scaled * upp * (1.0 + gate * (1.0 - sig))).astype(BF16), (scaled * gate).astype(BF16)


def kernel(tok, hgt, wt, ant, mot, ov, an, mo, x_v, xt, mbl, mfl, hg,
           wz, rsr, rss, rsr1, rss1, xr, xs, xr8, az, own, mb, gp,
           lsem, gs, gr, rs_s, rs_r, ag_s, ag_r, xx_s, xx_r, ax_s, ax_r):
    w = lax.axis_index("worker")
    f = lax.axis_index("fsdp")
    t = lax.axis_index("tensor")
    z, xh, y, core = w // 2, w % 2, f // 2, f % 2
    xo = 1 - xh

    def dev(dz=0, dx=0, dy=0, dc=0, dt=0):
        return (((z + dz + 8) % 8) * 2 + (xh + dx) % 2,
                ((y + dy + 4) % 4) * 2 + (core + dc) % 2, (t + dt) % 2)

    zdev = (dev(dz=1), dev(dz=-1))
    xdev = dev(dx=1)
    ydevs = (dev(dy=1), dev(dy=-1), dev(dy=2))
    cdev = dev(dc=1)
    tdev = dev(dt=1)

    barrier = pltpu.get_barrier_semaphore()
    for d in (*zdev, xdev, *ydevs, cdev, tdev):
        pl.semaphore_signal(barrier, inc=1, device_id=d, device_id_type=MESH)

    loads = []

    def load(src, dst, k):
        c = pltpu.make_async_copy(src, dst, lsem.at[k])
        c.start()
        loads.append(c)

    def rowblock(ff):
        return pl.ds(pl.multiple_of(ff * 128, 128), 128)

    def colblock(tt):
        return pl.ds(pl.multiple_of(tt * 1024, 128), 1024)

    load(tok, x_v.at[rowblock(f), colblock(t)], 0)
    for zz in range(8):
        load(wt.at[:, :, pl.ds(zz * 256, 256)], wz.at[zz], 1 + zz)
    load(ant, an, 9)
    load(mot, mo, 10)
    load(hgt, hg, 11)
    pl.semaphore_wait(barrier, 8)
    waited = []

    def need(*ks):
        for k in ks:
            if k not in waited:
                waited.append(k)
                loads[k].wait()

    sent = []

    def copy(src, dst, ssem, rsem, to):
        return pltpu.make_async_remote_copy(src_ref=src, dst_ref=dst, send_sem=ssem, recv_sem=rsem,
                                            device_id=to, device_id_type=MESH)

    def send(src, dst, ssem, rsem, to):
        c = copy(src, dst, ssem, rsem, to)
        c.start()
        sent.append(c)

    def arrived(ref, rsem):
        copy(ref, ref, ssem=gs.at[0], rsem=rsem, to=cdev).wait_recv()

    def piece(ff, tt):
        return x_v.at[rowblock(ff), colblock(tt)]

    to = 1 - t
    fy = [((y + dy + 4) % 4) * 2 + core for dy in (-1, 1, -2)]

    def g_own():
        p = piece(f, t)
        send(tok, p, gs.at[0], gr.at[0], tdev)
        for k in range(3):
            send(tok, p, gs.at[1 + k], gr.at[1 + k], ydevs[k])
        send(tok, p, gs.at[4], gr.at[4], cdev)

    def g_pair():
        p = piece(f, to)
        arrived(p, gr.at[0])
        for k in range(3):
            send(p, p, gs.at[5 + k], gr.at[5 + k], ydevs[k])
        send(p, p, gs.at[8], gr.at[8], cdev)

    def g_y(tt, k0, k1):
        for k in range(3):
            p = piece(fy[k], tt)
            arrived(p, gr.at[k0 + k])
            send(p, p, gs.at[k1 + k], gr.at[k1 + k], cdev)

    def g_end():
        fo = f + 1 - 2 * core
        arrived(piece(fo, t), gr.at[4])
        arrived(piece(fo, to), gr.at[8])
        for k in range(3):
            ff = fy[k] + 1 - 2 * core
            arrived(piece(ff, t), gr.at[9 + k])
            arrived(piece(ff, to), gr.at[12 + k])

    starts = [sum(r[0] for r in CHUNKS[:i]) for i in range(len(CHUNKS))]

    def lanes(h):
        return pl.ds(pl.multiple_of(h * 128, 128), 128)

    def zof(k):
        return (z + k + 16) % 8

    def run(c, name):
        R, rz, az_first, up = CHUNKS[c]
        rows = pl.ds(starts[c], R)
        dirs = ((0, 1, up), (1, -1, 7 - up))

        def f32(ref):
            return ref[...].astype(F32)

        if name == 0 and rz:
            pass
        else:
            need(*range(1, 9))
        if name == -1:
            send(wz.at[:, :, rows, lanes(xo)], xr8.at[:, :, rows], xx_s.at[c], xx_r.at[c], xdev)
        elif 0 <= name <= 3:
            s = name
            if not rz and s == 0:
                arrived(xr8.at[:, :, rows], xx_r.at[c])
            for d, sg, n in dirs:
                if s >= n:
                    continue
                zo = zof(sg * (n - s))
                k = d * 4 + s
                if rz:
                    src = wz.at[zo, :, rows]
                    if s == 0:
                        src = wt.at[:, rows, pl.ds(pl.multiple_of(zo * 256, 256), 256)]
                    else:
                        got = rsr.at[k - 1, :, rows]
                        arrived(got, rs_r.at[c, k - 1])
                        rss[k, :, rows] = (f32(src) + f32(got)).astype(BF16)
                        src = rss.at[k, :, rows]
                    send(src, rsr.at[k, :, rows], rs_s.at[c, k], rs_r.at[c, k], zdev[d])
                else:
                    total = f32(wz.at[zo, :, rows, lanes(xh)]) + f32(xr8.at[zo, :, rows])
                    if s > 0:
                        got = rsr1.at[k - 1, :, rows]
                        arrived(got, rs_r.at[c, k - 1])
                        total = total + f32(got)
                    rss1[k, :, rows] = total.astype(BF16)
                    send(rss1.at[k, :, rows], rsr1.at[k, :, rows], rs_s.at[c, k], rs_r.at[c, k], zdev[d])
        elif name == 4:
            for d, sg, n in dirs:
                arrived(rsr.at[d * 4 + n - 1, :, rows], rs_r.at[c, d * 4 + n - 1])

            def part(h):
                return (f32(wz.at[z, :, rows, lanes(h)]) + f32(rsr.at[up - 1, :, rows, lanes(h)])
                        + f32(rsr.at[4 + 6 - up, :, rows, lanes(h)]))

            xs[:, rows] = part(xo).astype(BF16)
            send(xs.at[:, rows], xr.at[:, rows], xx_s.at[c], xx_r.at[c], xdev)
            own[:, rows] = part(xh)
        elif name == 5:
            if rz:
                arrived(xr.at[:, rows], xx_r.at[c])
                total = own[:, rows] + f32(xr.at[:, rows])
            else:
                for d, sg, n in dirs:
                    arrived(rsr1.at[d * 4 + n - 1, :, rows], rs_r.at[c, d * 4 + n - 1])
                total = (f32(wz.at[z, :, rows, lanes(xh)]) + f32(xr8.at[z, :, rows])
                         + f32(rsr1.at[up - 1, :, rows]) + f32(rsr1.at[4 + 6 - up, :, rows]))
            anchor = an[:, rows]
            pseudo = anchor - total * (1.0 / WORKERS)
            mom = MOMENTUM_RATE * mo[:, rows] + pseudo
            new = anchor - OUTER_RATE * (pseudo + MOMENTUM_RATE * mom)
            mo[:, rows] = mom
            an[:, rows] = new
            az[z, xh, :, rows] = new.astype(BF16)
            mine = az.at[z, xh, :, rows]
            send(mine, mine, ax_s.at[c, 0], ax_r.at[c], xdev)
            if az_first:
                for d, sg, n in dirs:
                    send(mine, mine, ag_s.at[c, d * 4], ag_r.at[c, d * 4], zdev[d])
        elif 6 <= name <= 10:
            s = name - 6
            if not az_first and s == 0:
                arrived(az.at[z, xo, :, rows], ax_r.at[c])
            for d, sg, n in dirs:
                if s > n or (s == n and not az_first):
                    continue
                zo = zof(-sg * s)
                if az_first:
                    blk = az.at[zo, xh, :, rows]
                else:
                    blk = az.at[zo, :, :, rows]
                if s > 0:
                    arrived(blk, ag_r.at[c, d * 4 + s - 1])
                if s < n:
                    send(blk, blk, ag_s.at[c, d * 4 + s], ag_r.at[c, d * 4 + s], zdev[d])
                if az_first:
                    send(blk, blk, ax_s.at[c, d * up + s], ax_r.at[c], xdev)
        elif name == 11:
            if az_first:
                arrived(az.at[:, xo, :, rows], ax_r.at[c])
            else:
                for d, sg, n in dirs:
                    arrived(az.at[zof(-sg * n), :, :, rows], ag_r.at[c, d * 4 + n - 1])

            for zz in range(8):
                for h in range(2):
                    for p in range(2):
                        m = MIX * f32(wz.at[zz, p, rows, pl.ds(h * 128, 128)]) + (1.0 - MIX) * f32(az.at[zz, h, p, rows])
                        to_row, to_col = pl.ds(p * R, R), pl.ds(zz * 256 + h * 128, 128)
                        if c == LAST:
                            mbl[to_row, to_col] = m.astype(BF16)
                            mfl[to_row, to_col] = m
                        else:
                            mb[to_row, to_col] = m.astype(BF16)
        elif name == 12:
            for i in range(4):
                tk = pl.ds(i * 256, 256)
                g = jnp.dot(mb[pl.ds(0, 2 * R), :], xt[:, tk], preferred_element_type=F32) * SCALE
                gp[pl.ds(0, R), tk], gp[pl.ds(R, R), tk] = pair_grad(g, hg[rows, tk].astype(F32), R)
        elif name == 13:
            for zz in range(8):
                cols = pl.ds(zz * 256, 256)
                wg = jnp.dot(gp[pl.ds(0, 2 * R), :], x_v[:, cols], preferred_element_type=F32) * SCALE
                for p in range(2):
                    for h in range(2):
                        m = MIX * f32(wz.at[zz, p, rows, pl.ds(h * 128, 128)]) + (1.0 - MIX) * f32(az.at[zz, h, p, rows])
                        ov[p, rows, pl.ds(zz * 256 + h * 128, 128)] = (
                            m - wg[p * R:(p + 1) * R, h * 128:(h + 1) * 128]).astype(BF16)

    for c, name in ORDER:
        if c == LAST and name > 11:
            continue
        if c >= 0:
            run(c, name)
            for _ in range(min(4, max(0, len(sent) - 40))):
                sent.pop(0).wait_send()
        elif name == 0:
            g_own()
        elif name == 1:
            g_pair()
        elif name == 2:
            g_y(t, 1, 9)
        elif name == 3:
            g_y(to, 5, 12)
        elif name == 4:
            g_end()
            need(0, 11)
        elif name == 5:
            need(9, 10)
        elif name >= 8:
            for i in (2 * name - 16, 2 * name - 15):
                xt[:, pl.ds(i * 128, 128)] = x_v[pl.ds(i * 128, 128), :].T

    for s in sent:
        s.wait_send()


def finish(ov, an, mo, x_v, xt, mbl, mfl, hg, upt, aot, mut, gp, ol, sem):
    R = LAST_ROWS
    end = FIRST_ROW + R
    rows = pl.ds(FIRST_ROW, R)
    moves = []
    for lo, n in ((0, FIRST_ROW), (end, FFL - end)):
        if n:
            moves.append((ov.at[:, pl.ds(lo, n)], upt.at[:, pl.ds(lo, n)]))
    moves += [(an, aot), (mo, mut)]
    copies = [pltpu.make_async_copy(src, dst, sem.at[k]) for k, (src, dst) in enumerate(moves)]
    for c in copies:
        c.start()
    for i in range(4):
        tk = pl.ds(i * 256, 256)
        g = jnp.dot(mbl[...], xt[:, tk], preferred_element_type=F32) * SCALE
        gp[pl.ds(0, R), tk], gp[pl.ds(R, R), tk] = pair_grad(g, hg[rows, tk].astype(F32), R)
    for zz in range(8):
        cols = pl.ds(zz * 256, 256)
        wg = jnp.dot(gp[...], x_v[:, cols], preferred_element_type=F32) * SCALE
        for p in range(2):
            ol[p, :, cols] = (mfl[pl.ds(p * R, R), cols] - wg[p * R:(p + 1) * R]).astype(BF16)
        if zz % 2 == 1:
            done = pl.ds(zz * 256 - 256, 512)
            last = pltpu.make_async_copy(ol.at[:, :, done], upt.at[:, rows, done], sem.at[4 + zz // 2])
            last.start()
            copies.append(last)
    for c in copies:
        c.wait()


def body(tokens, hidden_grad, local_weights, anchor, momentum):
    n = len(CHUNKS)
    most = max(r[0] for r in CHUNKS)
    dma = pltpu.SemaphoreType.DMA
    hbm = pl.BlockSpec(memory_space=pl.ANY)
    vmem = pl.BlockSpec(memory_space=pltpu.VMEM)
    held = pl.pallas_call(
        kernel,
        name="outer_inner_step",
        out_shape=(
            pltpu.VMEM((2, FFL, D), BF16),
            pltpu.VMEM((2, FFL, 128), F32),
            pltpu.VMEM((2, FFL, 128), F32),
            pltpu.VMEM((TOK, D), BF16),
            pltpu.VMEM((D, TOK), BF16),
            pltpu.VMEM((2 * LAST_ROWS, D), BF16),
            pltpu.VMEM((2 * LAST_ROWS, D), F32),
            pltpu.VMEM((FFL, TOK), BF16),
        ),
        in_specs=[hbm] * 5,
        out_specs=(vmem,) * 8,
        scratch_shapes=[
            pltpu.VMEM((8, 2, FFL, 256), BF16),
            pltpu.VMEM((8, 2, FFL, 256), BF16),
            pltpu.VMEM((8, 2, FFL, 256), BF16),
            pltpu.VMEM((8, 2, FFL, 128), BF16),
            pltpu.VMEM((8, 2, FFL, 128), BF16),
            pltpu.VMEM((2, FFL, 128), BF16),
            pltpu.VMEM((2, FFL, 128), BF16),
            pltpu.VMEM((8, 2, FFL, 128), BF16),
            pltpu.VMEM((8, 2, 2, FFL, 128), BF16),
            pltpu.VMEM((2, FFL, 128), F32),
            pltpu.VMEM((2 * most, D), BF16),
            pltpu.VMEM((2 * most, TOK), BF16),
            dma((12,)),
            dma((15,)), dma((15,)),
            dma((n, 8)), dma((n, 8)),
            dma((n, 8)), dma((n, 8)),
            dma((n,)), dma((n,)),
            dma((n, 8)), dma((n,)),
        ],
        compiler_params=pltpu.CompilerParams(
            collective_id=0, has_side_effects=True, vmem_limit_bytes=45 << 20),
        cost_estimate=pl.CostEstimate(flops=4 * TOK * 2 * FFL * D, bytes_accessed=11_000_000, transcendentals=TOK * FFL),
    )(
        tokens[0],
        hidden_grad[0].T,
        local_weights[0].transpose(1, 2, 0),
        anchor.transpose(1, 2, 0),
        momentum.transpose(1, 2, 0),
    )
    up, an, mo = pl.pallas_call(
        finish,
        name="finish",
        out_shape=(
            jax.ShapeDtypeStruct((2, FFL, D), BF16),
            jax.ShapeDtypeStruct((2, FFL, 128), F32),
            jax.ShapeDtypeStruct((2, FFL, 128), F32),
        ),
        in_specs=[vmem] * 8,
        out_specs=(hbm,) * 3,
        scratch_shapes=[
            pltpu.VMEM((2 * LAST_ROWS, TOK), BF16),
            pltpu.VMEM((2, LAST_ROWS, D), BF16),
            dma((8,)),
        ],
        compiler_params=pltpu.CompilerParams(vmem_limit_bytes=12 << 20),
    )(*(pltpu.with_memory_space_constraint(a, pltpu.VMEM) for a in held))
    return (up.transpose(2, 0, 1)[None], an.transpose(2, 0, 1), mo.transpose(2, 0, 1))


def solution(mesh):
    in_specs = (
        P("worker", "fsdp", "tensor"),
        P("worker", None, ("fsdp", "tensor")),
        P("worker", None, None, ("fsdp", "tensor")),
        P("worker", None, ("fsdp", "tensor")),
        P("worker", None, ("fsdp", "tensor")),
    )
    out_specs = (
        P("worker", None, None, ("fsdp", "tensor")),
        P("worker", None, ("fsdp", "tensor")),
        P("worker", None, ("fsdp", "tensor")),
    )
    return jax.shard_map(body, mesh=mesh, in_specs=in_specs, out_specs=out_specs, check_vma=False)
```
